256 devices in a mesh: cell: 16 (over x, y), sub: 16 (over z, core).
Axes of the slice: x: 4, y: 4, z: 8, core: 2. Of those that a mesh axis runs over, the one named last changes fastest.
Arguments:
- shell_conc: float32 [16, 64, 10, 256, 128], P('cell', 'sub'), may hold values from 0.2 to 0.8
- heat_rise: float32 [16, 30, 256, 128], P('cell', None, 'sub'), may hold values from -5 to 5
- layer_current: float32 [16, 64, 256, 128], P('cell', 'sub'), may hold values from -4 to 4
- layer_counts: int32 [16], replicated, may hold values from 1 to 4, 30 in all
- contacts: int32 [16, 2], replicated, may hold values from -1 to 15, as said below
Outputs:
- conc_new: float32 [16, 64, 10, 256, 128], P('cell', 'sub')
- heat_new: float32 [16, 30, 256, 128], P('cell', None, 'sub')
The draws below stay inside these ranges and needn't reach their ends.
Inputs may be any that keep to these rules, and one draw needn't show every extreme that they name: `layer_counts`: entry d is the number of consecutive layers held by index d of sub, in order; the entries sum to 30 and the largest is exactly 4. `contacts`: row c names the cell below and the cell above cell c in one stacking order of all 16 cells, each cell once; -1 marks the two ends of the stack.
All inputs are finite; a program needn't handle non-finite values.
Results may differ from the reference program's by a relative error of at most 0.0003.
Values sent between devices are 32-bit elements; how exact they have to be, the bound alone decides.
No kernel may reach another device: no remote copies, remote signals or barrier semaphores. Data moves between devices by JAX's collectives and lax.ppermute only.
A program may use at most 64 MiB of HBM per device.

```python
import math
import jax
import jax.numpy as jnp
import numpy as np
from jax import lax

LAYERS = 30
LSLOT = 4
SHELLS = 10
GX = 128
CELLS = 16
SUBS = 16
SLOTS = 64
GY = 256


def draw_contacts(key, part):
    stacking = jax.random.permutation(jax.random.fold_in(key, 11), CELLS).astype(jnp.int32)
    placing = jnp.zeros((CELLS,), jnp.int32).at[stacking].set(jnp.arange(CELLS, dtype=jnp.int32))
    padded = jnp.concatenate([jnp.full((1,), -1, jnp.int32), stacking, jnp.full((1,), -1, jnp.int32)])
    below_cell = padded[placing]
    above_cell = padded[placing + 2]
    return jnp.stack([below_cell, above_cell], axis=1).astype(jnp.int32)


def block_scale(stream_key, extent, shards, low, largest):
    factor_of = 1.0
    for dim, parts in shards:
        steps = jax.random.uniform(jax.random.fold_in(jax.random.fold_in(stream_key, 6), dim), (parts,), jnp.float32, low / len(shards), largest / len(shards))
        factor_of = factor_of * jnp.repeat(jnp.exp(steps), extent[dim] // parts).reshape((-1,) + (1,) * (len(extent) - 1 - dim))
    return factor_of


def length_profile(amount, total, bound, lean):
    weights = [(1 << 20) // math.isqrt(grade ** lean) + 1 for grade in range(2, amount + 1)]
    surplus, given = total - bound - (amount - 1), [1] * (amount - 1)
    while surplus > 0:
        candidates = [i for i in range(amount - 1) if given[i] < bound]
        pool, left = sum([weights[i] for i in candidates]), surplus
        for i in candidates:
            addition = min(bound - given[i], max(1, left * weights[i] // pool), surplus)
            given[i] = given[i] + addition
            surplus = surplus - addition
    return np.array([bound] + given)


def ragged_sizes(key, count, total, bound, slope):
    if count == 2:
        one = jax.random.randint(key, (), max(1, total - bound), min(bound, total - 1) + 1)
        return jnp.stack([one, total - one])
    lengths = jnp.asarray(length_profile(count, total, bound, slope), jnp.int32)
    twos = (count - 1) // 2
    source_of, sink = lengths[1:1 + 2 * twos:2], lengths[2:2 + 2 * twos:2]
    room = jnp.minimum(source_of - 1, bound - sink)
    moved = jax.random.randint(jax.random.fold_in(key, 1), (twos,), 0, 1 << 20) % (room + 1)
    lengths = lengths.at[1:1 + 2 * twos:2].set(source_of - moved).at[2:2 + 2 * twos:2].set(sink + moved)
    return lengths[jax.random.permutation(jax.random.fold_in(key, 2), count)]


def centred(stream_key, shape, scale, reach, cuts=(), kind=jnp.bfloat16):
    drawn = scale * jax.random.normal(stream_key, shape, jnp.float32)
    if cuts:
        drawn = drawn * block_scale(stream_key, shape, cuts, -0.22, 0.18)
    return jnp.clip(drawn, -reach, reach).astype(kind)


def setup_inputs(seed: int = 0) -> dict:
    key_of = jax.random.split(jax.random.key(seed), 6)
    return {
        "shell_conc": jnp.clip(0.2 + 0.6 * jax.random.uniform(key_of[0], (CELLS, SLOTS, SHELLS, GY, GX), jnp.float32) ** block_scale(key_of[0], (CELLS, SLOTS, SHELLS, GY, GX), ((0, 16), (1, 16)), -0.2, 0.2), 0.2, 0.8),
        "heat_rise": jnp.clip(jax.random.uniform(key_of[1], (CELLS, LAYERS, GY, GX), jnp.float32, -5.0, 5.0) * block_scale(key_of[1], (CELLS, LAYERS, GY, GX), ((0, 16), (2, 16)), -0.4, 0.0), -5.0, 5.0),
        "layer_current": centred(key_of[2], (CELLS, SLOTS, GY, GX), 1.0, 4.0, ((0, 16), (1, 16)), jnp.float32),
        "layer_counts": ragged_sizes(key_of[3], SUBS, LAYERS, LSLOT, 2).astype(jnp.int32),
        "contacts": draw_contacts(jax.random.fold_in(key_of[5], 71), 0),
    }


BASE_KELVIN = 298.15
RATE_ACTIVATION = 5000.0
DIFFUSION_ACTIVATION = 3000.0
RATE_CONSTANT = 0.5
VOLT_PER_KELVIN = 2.0 * 8.314462618 / 96485.33212
HEAT_SCALE = 10.0
ENTROPY_SLOPE = 0.001
DIFFUSION_STEP = 0.005
SURFACE_STEP = 0.005
INPLANE_CONDUCT = 0.25
THROUGH_CONDUCT = 2.0
CONTACT_CONDUCT = 0.5

def inverse_sine(value):
    magnitude = jnp.abs(value)
    rooted = jnp.sqrt(1.0 + magnitude * magnitude)
    positive = jnp.log1p(magnitude + magnitude * magnitude / (1.0 + rooted))
    return jnp.where(value < 0.0, -positive, positive)

def layer_tables(layer_counts, slot_count, layer_total):
    counts = layer_counts.astype(jnp.int32)
    finish = jnp.cumsum(counts).astype(jnp.int32)
    starts = (finish - counts).astype(jnp.int32)
    devices = counts.shape[0]
    device_ids = jnp.arange(devices, dtype=jnp.int32)
    slot_index = jnp.arange(devices * slot_count, dtype=jnp.int32)
    slot_owner = slot_index // slot_count
    slot_place = slot_index % slot_count
    owner_hits = slot_owner[:, None] == device_ids[None, :]
    owner_count = lax.optimization_barrier(jnp.sum(jnp.where(owner_hits, counts[None, :], 0), axis=1)).astype(jnp.int32)
    owner_start = lax.optimization_barrier(jnp.sum(jnp.where(owner_hits, starts[None, :], 0), axis=1)).astype(jnp.int32)
    live_slot = slot_place < owner_count
    slot_layer = jnp.minimum(owner_start + slot_place, layer_total - 1).astype(jnp.int32)
    layer_index = jnp.arange(layer_total, dtype=jnp.int32)
    layer_owner = lax.optimization_barrier(jnp.sum((finish[None, :] <= layer_index[:, None]).astype(jnp.int32), axis=1)).astype(jnp.int32)
    layer_hits = layer_owner[:, None] == device_ids[None, :]
    layer_start = lax.optimization_barrier(jnp.sum(jnp.where(layer_hits, starts[None, :], 0), axis=1)).astype(jnp.int32)
    layer_slot = (layer_owner * slot_count + layer_index - layer_start).astype(jnp.int32)
    return (live_slot, slot_layer, layer_slot)

def kinetics(surface, kelvin, current):
    reciprocal = 1.0 / BASE_KELVIN - 1.0 / kelvin
    base_rate = RATE_CONSTANT * jnp.exp(RATE_ACTIVATION * reciprocal) * jnp.sqrt(surface * (1.0 - surface))
    ratio_rate = current / (2.0 * base_rate)
    arcsine = inverse_sine(ratio_rate)
    overvoltage = VOLT_PER_KELVIN * kelvin * arcsine
    entropic = ENTROPY_SLOPE * (0.5 - surface)
    source = HEAT_SCALE * current * (overvoltage + kelvin * entropic)
    heat_slope = HEAT_SCALE * current * (VOLT_PER_KELVIN * arcsine - VOLT_PER_KELVIN * ratio_rate * RATE_ACTIVATION / (kelvin * jnp.sqrt(1.0 + ratio_rate * ratio_rate)) + entropic)
    return (source, heat_slope)

def particle(states, kelvin, current):
    shells = states.shape[1]
    speedup = jnp.exp(DIFFUSION_ACTIVATION * (1.0 / BASE_KELVIN - 1.0 / kelvin))
    volumes = [((radial + 1) ** 3 - radial ** 3) / (3.0 * shells ** 3) for radial in range(shells)]
    linkage = [DIFFUSION_STEP * speedup * ((radial + 1) ** 2 / shells ** 2 * shells) for radial in range(shells - 1)]
    uppers = []
    values = []
    for radial in range(shells):
        diagonal = volumes[radial] + jnp.zeros_like(kelvin)
        right_side = volumes[radial] * states[:, radial]
        if radial < shells - 1:
            diagonal = diagonal + linkage[radial]
        else:
            right_side = right_side - SURFACE_STEP * current
        if radial > 0:
            diagonal = diagonal + linkage[radial - 1] - linkage[radial - 1] * uppers[radial - 1]
            right_side = right_side + linkage[radial - 1] * values[radial - 1]
        if radial < shells - 1:
            uppers.append(linkage[radial] / diagonal)
        else:
            uppers.append(jnp.zeros_like(kelvin))
        values.append(right_side / diagonal)
    result = [None] * shells
    result[shells - 1] = values[shells - 1]
    for radial in range(shells - 2, -1, -1):
        result[radial] = values[radial] + uppers[radial] * result[radial + 1]
    return jnp.stack(result, axis=1)

def column_solve(right_side, heat_slope):
    layer_total = right_side.shape[1]
    uppers = []
    values = []
    for height in range(layer_total):
        diagonal = 1.0 - heat_slope[:, height]
        source = right_side[:, height]
        if height > 0:
            diagonal = diagonal + THROUGH_CONDUCT - THROUGH_CONDUCT * uppers[height - 1]
            source = source + THROUGH_CONDUCT * values[height - 1]
        if height < layer_total - 1:
            diagonal = diagonal + THROUGH_CONDUCT
        uppers.append(THROUGH_CONDUCT / diagonal)
        values.append(source / diagonal)
    result = [None] * layer_total
    result[layer_total - 1] = values[layer_total - 1]
    for height in range(layer_total - 2, -1, -1):
        result[height] = values[height] + uppers[height] * result[height + 1]
    return jnp.stack(result, axis=1)

def reference(shell_conc, heat_rise, layer_current, layer_counts, contacts):
    live_slot, slot_layer, layer_slot = layer_tables(layer_counts, LSLOT, LAYERS)
    slot_rise = jnp.take(heat_rise, slot_layer, axis=1)
    kelvin = BASE_KELVIN + slot_rise
    surface = shell_conc[:, :, SHELLS - 1]
    source, heat_slope = kinetics(surface, kelvin, layer_current)

    def per_cell(operands):
        return particle(operands[0], operands[1], operands[2])
    updated = lax.map(per_cell, (shell_conc, kelvin, layer_current))
    conc_new = jnp.where(live_slot[None, :, None, None, None], updated, 0.0)
    layer_source = jnp.take(source, layer_slot, axis=1)
    layer_slope = jnp.take(heat_slope, layer_slot, axis=1)
    lower_cell = contacts[:, 0]
    upper_cell = contacts[:, 1]
    below_face = jnp.where((lower_cell >= 0)[:, None, None], jnp.take(heat_rise[:, LAYERS - 1], jnp.maximum(lower_cell, 0), axis=0), 0.0)
    above_face = jnp.where((upper_cell >= 0)[:, None, None], jnp.take(heat_rise[:, 0], jnp.maximum(upper_cell, 0), axis=0), 0.0)
    padded = jnp.pad(heat_rise, ((0, 0), (0, 0), (1, 1), (1, 1)), mode='edge')
    laplace = padded[:, :, 2:, 1:-1] + padded[:, :, :-2, 1:-1] + padded[:, :, 1:-1, 2:] + padded[:, :, 1:-1, :-2] - 4.0 * heat_rise
    right_side = heat_rise + INPLANE_CONDUCT * laplace + layer_source - layer_slope * heat_rise
    first_row = right_side[:, 0] + CONTACT_CONDUCT * (below_face - heat_rise[:, 0])
    last_row = right_side[:, LAYERS - 1] + CONTACT_CONDUCT * (above_face - heat_rise[:, LAYERS - 1])
    right_side = jnp.concatenate([first_row[:, None], right_side[:, 1:LAYERS - 1], last_row[:, None]], axis=1)
    heat_new = column_solve(right_side, layer_slope)
    return (conc_new, heat_new)
```

```python
import functools

import jax
import jax.numpy as jnp
from jax import lax
from jax.experimental import pallas as pl
from jax.experimental.pallas import tpu as pltpu
from jax.sharding import PartitionSpec as P

BASE_KELVIN = 298.15
RATE_ACTIVATION = 5000.0
DIFFUSION_ACTIVATION = 3000.0
RATE_CONSTANT = 0.5
VOLT_PER_KELVIN = 2.0 * 8.314462618 / 96485.33212
HEAT_SCALE = 10.0
ENTROPY_SLOPE = 0.001
DIFFUSION_STEP = 0.005
SURFACE_STEP = 0.005
INPLANE_CONDUCT = 0.25
THROUGH_CONDUCT = 2.0
CONTACT_CONDUCT = 0.5

SMEM = pltpu.MemorySpace.SMEM
VMEM = pltpu.MemorySpace.VMEM


def reciprocal(value):
    guess = pl.reciprocal(value, approx=True)
    return guess * (2.0 - value * guess)


def starts_of(counts_ref, devices):
    starts = [jnp.int32(0)]
    for d in range(devices):
        starts.append(starts[-1] + counts_ref[d])
    return starts


def pack_rise(heat_rise, layer_counts, slots):
    layers, rows, columns = heat_rise.shape
    devices = layer_counts.shape[0]

    def kernel(counts_ref, heat_ref, send_ref, low_ref, high_ref):
        starts = starts_of(counts_ref, devices)
        for d in range(devices):
            for s in range(slots):
                layer = jnp.minimum(starts[d] + s, layers - 1)
                send_ref[d * slots + s] = heat_ref[layer]
        for layer in range(layers):
            low_ref[layer : layer + 1] = heat_ref[layer, 0:1]
            high_ref[layer : layer + 1] = heat_ref[layer, rows - 1 : rows]

    edge = jax.ShapeDtypeStruct((layers, columns), jnp.float32)
    return pl.pallas_call(
        kernel,
        name="pack_rise",
        out_shape=(
            jax.ShapeDtypeStruct((devices * slots, rows, columns), jnp.float32),
            edge,
            edge,
        ),
        in_specs=[pl.BlockSpec(memory_space=SMEM), pl.BlockSpec(memory_space=VMEM)],
        out_specs=[pl.BlockSpec(memory_space=VMEM)] * 3,
    )(layer_counts, heat_rise)


def pack_kinetic(shell_conc, layer_current, devices):
    slots, shells, rows, columns = shell_conc.shape
    part = rows // devices

    def kernel(shell_ref, current_ref, send_ref, sem):
        copies = []
        for d in range(devices):
            here = pl.ds(d * part, part)
            copies.append(
                pltpu.make_async_copy(shell_ref.at[:, shells - 1, here], send_ref.at[d, 0], sem.at[2 * d])
            )
            copies.append(
                pltpu.make_async_copy(current_ref.at[:, here], send_ref.at[d, 1], sem.at[2 * d + 1])
            )
        for copy in copies:
            copy.start()
        for copy in copies:
            copy.wait()

    return pl.pallas_call(
        kernel,
        name="pack_kinetic",
        out_shape=jax.ShapeDtypeStruct((devices, 2, slots, part, columns), jnp.float32),
        in_specs=[pl.BlockSpec(memory_space=pl.ANY)] * 2,
        out_specs=pl.BlockSpec(memory_space=VMEM),
        scratch_shapes=[pltpu.SemaphoreType.DMA((2 * devices,))],
    )(shell_conc, layer_current)


def particle(shell_conc, slot_rise, layer_current, layer_counts, chunk=32):
    slots, shells, rows, columns = shell_conc.shape
    sources, _, part, _ = slot_rise.shape
    halves = 2
    block = rows // halves
    volume = [((i + 1) ** 3 - i**3) / (3.0 * shells**3) for i in range(shells)]
    link = [DIFFUSION_STEP * ((i + 1) ** 2 / shells**2 * shells) for i in range(shells - 1)]

    def kernel(counts_ref, shell_ref, rise_ref, current_ref, out_ref):
        live = pl.program_id(0) < counts_ref[lax.axis_index("sub")]

        @pl.when(jnp.logical_not(live))
        def _():
            out_ref[...] = jnp.zeros_like(out_ref)

        @pl.when(live)
        def _():
            for c in range(block // chunk):
                here = slice(c * chunk, (c + 1) * chunk)
                rise = jnp.concatenate(
                    [rise_ref[c * chunk // part + k, 0] for k in range(chunk // part)], axis=0
                )
                scaled = rise * (DIFFUSION_ACTIVATION / BASE_KELVIN)
                speedup = jnp.exp(scaled * reciprocal(BASE_KELVIN + rise))
                held = [None] * shells
                inverse = [None] * shells
                capacity = amount = None
                for i in range(shells):
                    gain = volume[i] * shell_ref[0, i, here]
                    if i == 0:
                        capacity, amount = volume[0], gain
                    else:
                        capacity = volume[i] + upper * capacity
                        amount = gain + upper * amount
                    if i < shells - 1:
                        flow = link[i] * speedup
                        inverse[i] = reciprocal(capacity + flow)
                        upper = flow * inverse[i]
                    else:
                        amount = amount - SURFACE_STEP * current_ref[0, here]
                        inverse[i] = reciprocal(capacity)
                    held[i] = amount
                value = held[-1] * inverse[-1]
                out_ref[0, shells - 1, here] = value
                for i in range(shells - 2, -1, -1):
                    value = inverse[i] * (held[i] + (link[i] * speedup) * value)
                    out_ref[0, i, here] = value

    return pl.pallas_call(
        kernel,
        name="particle",
        grid=(slots, halves),
        out_shape=jax.ShapeDtypeStruct(shell_conc.shape, jnp.float32),
        in_specs=[
            pl.BlockSpec(memory_space=SMEM),
            pl.BlockSpec((1, shells, block, columns), lambda s, h: (s, 0, h, 0)),
            pl.BlockSpec((sources // halves, 1, part, columns), lambda s, h: (h, s, 0, 0)),
            pl.BlockSpec((1, block, columns), lambda s, h: (s, h, 0)),
        ],
        out_specs=pl.BlockSpec((1, shells, block, columns), lambda s, h: (s, 0, h, 0)),
        cost_estimate=pl.CostEstimate(
            flops=20 * slots * shells * rows * columns,
            bytes_accessed=8 * slots * shells * rows * columns,
            transcendentals=0,
        ),
    )(layer_counts, shell_conc, slot_rise, layer_current)


def inverse_sine(value):
    magnitude = jnp.abs(value)
    rooted = jnp.sqrt(1.0 + magnitude * magnitude)
    positive = jnp.log1p(magnitude + magnitude * magnitude / (1.0 + rooted))
    return jnp.where(value < 0.0, -positive, positive), rooted


def column(heat_rise, kinetic, low, high, faces, layer_counts, contacts):
    layers, rows, columns = heat_rise.shape
    devices = layer_counts.shape[0]
    slots = kinetic.shape[0] // (2 * devices)
    last = layers - 1

    def kernel(counts_ref, contacts_ref, heat_ref, kinetic_ref, low_ref, high_ref, faces_ref, out_ref, place, slope_ref, right_ref):
        position = lax.axis_index("sub")
        cell = lax.axis_index("cell")
        starts = starts_of(counts_ref, devices)
        for d in range(devices):
            for s in range(slots):
                place[starts[d] + s] = 2 * slots * d + s
        row_id = lax.broadcasted_iota(jnp.int32, (rows, columns), 0)
        lane_id = lax.broadcasted_iota(jnp.int32, (rows, columns), 1)
        for layer in range(layers):
            rise = heat_ref[layer]
            low_row = jnp.where(position == 0, rise[0:1], low_ref[layer : layer + 1])
            high_row = jnp.where(position == devices - 1, rise[rows - 1 : rows], high_ref[layer : layer + 1])
            laplace = (
                jnp.where(row_id == 0, low_row, pltpu.roll(rise, 1, 0))
                + jnp.where(row_id == rows - 1, high_row, pltpu.roll(rise, rows - 1, 0))
                + jnp.where(lane_id == 0, rise, pltpu.roll(rise, 1, 1))
                + jnp.where(lane_id == columns - 1, rise, pltpu.roll(rise, columns - 1, 1))
                - 4.0 * rise
            )
            where = place[layer]
            surface = kinetic_ref[where]
            current = kinetic_ref[where + slots]
            kelvin = BASE_KELVIN + rise
            inverse_kelvin = 1.0 / kelvin
            base_rate = (
                RATE_CONSTANT
                * jnp.exp((RATE_ACTIVATION / BASE_KELVIN) * rise * inverse_kelvin)
                * jnp.sqrt(surface * (1.0 - surface))
            )
            ratio_rate = current / (2.0 * base_rate)
            arcsine, rooted = inverse_sine(ratio_rate)
            entropic = ENTROPY_SLOPE * (0.5 - surface)
            drive = VOLT_PER_KELVIN * arcsine + entropic
            scaled = HEAT_SCALE * current
            source = scaled * (kelvin * drive)
            slope = scaled * (
                drive - (VOLT_PER_KELVIN * RATE_ACTIVATION) * ratio_rate * inverse_kelvin / rooted
            )
            right = rise + INPLANE_CONDUCT * laplace + source - slope * rise
            if layer == 0 or layer == last:
                side = 0 if layer == 0 else 1
                partner = contacts_ref[cell, side]
                face = faces_ref[jnp.maximum(partner, 0) ^ cell, 1 - side]
                face = jnp.where(partner >= 0, face, 0.0)
                right = right + CONTACT_CONDUCT * (face - rise)
            slope_ref[layer] = slope
            right_ref[layer] = right
        upper = value = None
        for layer in range(layers):
            diagonal = 1.0 - slope_ref[layer]
            source = right_ref[layer]
            if layer > 0:
                diagonal = diagonal + THROUGH_CONDUCT - THROUGH_CONDUCT * upper
                source = source + THROUGH_CONDUCT * value
            if layer < last:
                diagonal = diagonal + THROUGH_CONDUCT
            inverse = 1.0 / diagonal
            upper = THROUGH_CONDUCT * inverse
            value = source * inverse
            slope_ref[layer] = upper
            right_ref[layer] = value
        out_ref[last] = value
        for layer in range(last - 1, -1, -1):
            value = right_ref[layer] + slope_ref[layer] * value
            out_ref[layer] = value

    return pl.pallas_call(
        kernel,
        name="column",
        out_shape=jax.ShapeDtypeStruct(heat_rise.shape, jnp.float32),
        in_specs=[pl.BlockSpec(memory_space=SMEM)] * 2 + [pl.BlockSpec(memory_space=VMEM)] * 5,
        out_specs=pl.BlockSpec(memory_space=VMEM),
        scratch_shapes=[
            pltpu.SMEM((layers + slots,), jnp.int32),
            pltpu.VMEM((layers, rows, columns), jnp.float32),
            pltpu.VMEM((layers, rows, columns), jnp.float32),
        ],
        cost_estimate=pl.CostEstimate(
            flops=200 * layers * rows * columns, bytes_accessed=8 * layers * rows * columns, transcendentals=0
        ),
    )(layer_counts, contacts, heat_rise, kinetic, low, high, faces)


def per_device(shell_conc, heat_rise, layer_current, layer_counts, contacts):
    shell_conc, heat_rise, layer_current = shell_conc[0], heat_rise[0], layer_current[0]
    slots = shell_conc.shape[0]
    layers, part, columns = heat_rise.shape
    devices = lax.axis_size("sub")
    cells = lax.axis_size("cell")
    send_rise, low_edge, high_edge = pack_rise(heat_rise, layer_counts, slots)
    send_kinetic = pack_kinetic(shell_conc, layer_current, devices)
    got_rise = lax.all_to_all(send_rise.reshape(devices, slots, part, columns), "sub", 0, 0)
    got_kinetic = lax.all_to_all(send_kinetic, "sub", 0, 0)
    low = lax.ppermute(high_edge, "sub", [(i, i + 1) for i in range(devices - 1)])
    high = lax.ppermute(low_edge, "sub", [(i + 1, i) for i in range(devices - 1)])
    faces = jnp.stack([heat_rise[0], heat_rise[layers - 1]])[None]
    step = 1
    while step < cells:
        other = lax.ppermute(faces, "cell", [(i, i ^ step) for i in range(cells)])
        faces = jnp.concatenate([faces, other], axis=0)
        step *= 2
    conc_new = particle(shell_conc, got_rise, layer_current, layer_counts)
    heat_new = column(
        heat_rise, got_kinetic.reshape(-1, part, columns), low, high, faces, layer_counts, contacts
    )
    return conc_new[None], heat_new[None]


def solution(mesh):
    in_specs = (
        P("cell", "sub", None, None, None),
        P("cell", None, "sub", None),
        P("cell", "sub", None, None),
        P(),
        P(),
    )
    out_specs = (P("cell", "sub", None, None, None), P("cell", None, "sub", None))
    return jax.shard_map(
        per_device, mesh=mesh, in_specs=in_specs, out_specs=out_specs, check_vma=False
    )
```

```python
import functools

import jax
import jax.numpy as jnp
from jax import lax
from jax.experimental import pallas as pl
from jax.experimental.pallas import tpu as pltpu
from jax.sharding import PartitionSpec as P

BASE_KELVIN = 298.15
RATE_ACTIVATION = 5000.0
DIFFUSION_ACTIVATION = 3000.0
RATE_CONSTANT = 0.5
VOLT_PER_KELVIN = 2.0 * 8.314462618 / 96485.33212
HEAT_SCALE = 10.0
ENTROPY_SLOPE = 0.001
DIFFUSION_STEP = 0.005
SURFACE_STEP = 0.005
INPLANE_CONDUCT = 0.25
THROUGH_CONDUCT = 2.0
CONTACT_CONDUCT = 0.5

SMEM = pltpu.MemorySpace.SMEM
VMEM = pltpu.MemorySpace.VMEM
HBM = pltpu.MemorySpace.HBM


def reciprocal(value):
    return pl.reciprocal(value, approx=True)


def near(*arrays):
    return [pltpu.with_memory_space_constraint(array, VMEM) for array in arrays]


def far(*arrays):
    return [pltpu.with_memory_space_constraint(array, HBM) for array in arrays]


def params(mebibytes):
    return pltpu.CompilerParams(vmem_limit_bytes=mebibytes * 2**20)


def starts_of(counts_ref, devices):
    starts = [jnp.int32(0)]
    for d in range(devices):
        starts.append(starts[-1] + counts_ref[d])
    return starts


def pack_rise(heat_rise, layer_counts, contacts, slots):
    layers, rows, columns = heat_rise.shape
    devices = layer_counts.shape[0]
    cells = contacts.shape[1]

    def kernel(counts_ref, contacts_ref, heat_ref, send_ref, faces_ref):
        cell = lax.axis_index("cell")
        starts = starts_of(counts_ref, devices)
        for d in range(devices):
            for s in range(slots):
                layer = jnp.minimum(starts[d] + s, layers - 1)
                send_ref[d, s] = heat_ref[layer]
        for j in range(cells):
            faces_ref[j] = heat_ref[jnp.where(contacts_ref[0, j] == cell, layers - 1, 0)]

    return pl.pallas_call(
        kernel,
        name="pack_rise",
        out_shape=(
            VMEM((devices, slots, rows, columns), jnp.float32),
            VMEM((cells, rows, columns), jnp.float32),
        ),
        compiler_params=params(4),
        in_specs=[pl.BlockSpec(memory_space=SMEM)] * 2 + [pl.BlockSpec(memory_space=VMEM)],
        out_specs=[pl.BlockSpec(memory_space=VMEM)] * 2,
    )(layer_counts, contacts, *near(heat_rise))


def split_kinetic(shell_conc, layer_current, heat_rise, chips):
    slots, shells, rows, columns = shell_conc.shape
    layers, part, _ = heat_rise.shape
    blocks = chips * 2 * slots
    edges = -(-layers // part)

    def kernel(shell_ref, current_ref, heat_ref, mine_ref, theirs_ref, sem):
        core = lax.axis_index("sub") % 2
        copies = []
        for chip in range(chips):
            for turn, target in enumerate((theirs_ref, mine_ref)):
                side = 1 - core if turn == 0 else core
                here = pl.ds(pl.multiple_of((2 * chip + side) * part, part), part)
                for array, source in enumerate((shell_ref.at[:, shells - 1, here], current_ref.at[:, here])):
                    there = target.at[pl.ds((2 * chip + array) * slots, slots)]
                    copies.append(pltpu.make_async_copy(source, there, sem.at[len(copies)]))
        for copy in copies:
            copy.start()
        for layer in range(layers):
            block, row = layer // part, layer % part
            theirs_ref[blocks + block, row : row + 1] = heat_ref[layer, 0:1]
            theirs_ref[blocks + edges + block, row : row + 1] = heat_ref[layer, part - 1 : part]
        for copy in copies:
            copy.wait()

    return pl.pallas_call(
        kernel,
        name="split_kinetic",
        out_shape=(
            VMEM((blocks, part, columns), jnp.float32),
            VMEM((blocks + 2 * edges, part, columns), jnp.float32),
        ),
        compiler_params=params(4),
        in_specs=[pl.BlockSpec(memory_space=HBM)] * 2 + [pl.BlockSpec(memory_space=VMEM)],
        out_specs=[pl.BlockSpec(memory_space=VMEM)] * 2,
        scratch_shapes=[pltpu.SemaphoreType.DMA((4 * chips,))],
    )(*far(shell_conc, layer_current), *near(heat_rise))


def pack_kinetic(mine, got, hops):
    blocks, part, columns = mine.shape
    edges = (got.shape[0] - blocks) // 2
    chips = lax.axis_size("sub") // 2
    each = blocks // chips

    def kernel(mine_ref, got_ref, *send_refs):
        position = lax.axis_index("sub")
        chip, core = position // 2, position % 2
        for hop, send_ref in zip(hops, send_refs):
            target = lax.rem(chip + hop + chips, chips)
            send_ref[pl.ds(core * each, each)] = mine_ref[pl.ds(target * each, each)]
            send_ref[pl.ds((1 - core) * each, each)] = got_ref[pl.ds(target * each, each)]
            if abs(hop) == 1:
                first = blocks + (edges if hop == 1 else 0)
                send_ref[2 * each : 2 * each + edges] = got_ref[first : first + edges]

    return pl.pallas_call(
        kernel,
        name="pack_kinetic",
        out_shape=tuple(
            VMEM((2 * each + (edges if abs(hop) == 1 else 0), part, columns), jnp.float32)
            for hop in hops
        ),
        compiler_params=params(4),
        in_specs=[pl.BlockSpec(memory_space=VMEM)] * 2,
        out_specs=[pl.BlockSpec(memory_space=VMEM)] * len(hops),
    )(*near(mine, got))


def particle(shell_conc, slot_rise, layer_current, layer_counts, pieces=2, chunk=64):
    slots, shells, rows, columns = shell_conc.shape
    sources, _, part, _ = slot_rise.shape
    piece = rows // pieces
    volume = [((i + 1) ** 3 - i**3) / (3.0 * shells**3) for i in range(shells)]
    link = [DIFFUSION_STEP * ((i + 1) ** 2 / shells**2 * shells) for i in range(shells - 1)]

    def kernel(counts_ref, states_ref, rise_ref, current_ref, out_ref, shell_ref, made, sem, got_sem):
        fetches = [
            pltpu.make_async_copy(states_ref.at[slot], shell_ref.at[slot], got_sem.at[slot])
            for slot in range(slots)
        ]
        for fetch in fetches:
            fetch.start()
        count = counts_ref[lax.axis_index("sub")]

        def solve(slot, first):
            here = slice(first, first + chunk)
            rise = jnp.concatenate(
                [rise_ref[first // part + k, slot] for k in range(chunk // part)], axis=0
            )
            scaled = rise * (DIFFUSION_ACTIVATION / BASE_KELVIN)
            speedup = jnp.exp(scaled * reciprocal(BASE_KELVIN + rise))
            held = [None] * shells
            inverse = [None] * shells
            capacity = amount = upper = None
            for i in range(shells):
                gain = volume[i] * shell_ref[slot, i, here]
                if i == 0:
                    capacity, amount = volume[0], gain
                else:
                    capacity = volume[i] + upper * capacity
                    amount = gain + upper * amount
                if i < shells - 1:
                    flow = link[i] * speedup
                    inverse[i] = reciprocal(capacity + flow)
                    upper = flow * inverse[i]
                else:
                    amount = amount - SURFACE_STEP * current_ref[slot, here]
                    inverse[i] = reciprocal(capacity)
                held[i] = amount
            value = held[-1] * inverse[-1]
            made[slot, shells - 1, here] = value
            for i in range(shells - 2, -1, -1):
                value = inverse[i] * (held[i] + (link[i] * speedup) * value)
                made[slot, i, here] = value

        copies = []
        for slot in range(slots):
            fetches[slot].wait()
            for first in range(0, rows, piece):
                here = slice(first, first + piece)

                @pl.when(slot < count)
                def _(slot=slot, first=first):
                    for begin in range(first, first + piece, chunk):
                        solve(slot, begin)

                @pl.when(slot >= count)
                def _(slot=slot, here=here):
                    made[slot, :, here] = jnp.zeros((shells, piece, columns), jnp.float32)

                copies.append(
                    pltpu.make_async_copy(made.at[slot, :, here], out_ref.at[slot, :, here], sem.at[len(copies)])
                )
                copies[-1].start()
        for copy in copies:
            copy.wait()

    return pl.pallas_call(
        kernel,
        name="particle",
        out_shape=HBM(shell_conc.shape, jnp.float32),
        in_specs=[pl.BlockSpec(memory_space=SMEM), pl.BlockSpec(memory_space=HBM)]
        + [pl.BlockSpec(memory_space=VMEM)] * 2,
        out_specs=pl.BlockSpec(memory_space=HBM),
        scratch_shapes=[
            pltpu.VMEM(shell_conc.shape, jnp.float32),
            pltpu.VMEM(shell_conc.shape, jnp.float32),
            pltpu.SemaphoreType.DMA((slots * pieces,)),
            pltpu.SemaphoreType.DMA((slots,)),
        ],
        compiler_params=params(16),
        cost_estimate=pl.CostEstimate(
            flops=20 * slots * shells * rows * columns,
            bytes_accessed=8 * slots * shells * rows * columns,
            transcendentals=0,
        ),
    )(layer_counts, *far(shell_conc), *near(slot_rise, layer_current))


def inverse_sine(value):
    magnitude = jnp.abs(value)
    rooted = jnp.sqrt(1.0 + magnitude * magnitude)
    positive = jnp.log1p(magnitude + magnitude * magnitude / (1.0 + rooted))
    return jnp.where(value < 0.0, -positive, positive), rooted


def column(heat_rise, mine, got, arrived, hops, faces, after, layer_counts, contacts):
    layers, rows, columns = heat_rise.shape
    devices = layer_counts.shape[0]
    chips = devices // 2
    each = mine.shape[0] // chips
    slots = each // 2
    edges = -(-layers // rows)
    blocks = mine.shape[0]
    last = layers - 1

    def kernel(counts_ref, contacts_ref, _, heat_ref, mine_ref, got_ref, faces_ref, *refs):
        arrived_refs, (out_ref, place, kinetic_ref, slope_ref, right_ref) = refs[: len(hops)], refs[len(hops) :]
        position = lax.axis_index("sub")
        cell = lax.axis_index("cell")
        chip, core = position // 2, position % 2
        kinetic_ref[pl.ds(core * each, each)] = mine_ref[pl.ds(chip * each, each)]
        kinetic_ref[pl.ds((1 - core) * each, each)] = got_ref[pl.ds(chip * each, each)]
        for hop, ref in zip(hops, arrived_refs):
            kinetic_ref[hop % chips * 2 * each : (hop % chips + 1) * 2 * each] = ref[: 2 * each]
        starts = starts_of(counts_ref, devices)
        for d in range(devices):
            hop = lax.rem(chip - d // 2 + chips, chips)
            for s in range(slots):
                place[starts[d] + s] = (2 * hop + d % 2) * each + s
        from_low, from_high = arrived_refs[hops.index(1)], arrived_refs[hops.index(-1)]
        row_id = lax.broadcasted_iota(jnp.int32, (rows, columns), 0)
        lane_id = lax.broadcasted_iota(jnp.int32, (rows, columns), 1)
        for layer in range(layers):
            rise = heat_ref[layer]
            block, row = layer // rows, slice(layer % rows, layer % rows + 1)
            low_row = jnp.where(
                core == 0, from_low[2 * each + block, row], got_ref[blocks + edges + block, row]
            )
            high_row = jnp.where(core == 0, got_ref[blocks + block, row], from_high[2 * each + block, row])
            low_row = jnp.where(position == 0, rise[0:1], low_row)
            high_row = jnp.where(position == devices - 1, rise[rows - 1 : rows], high_row)
            laplace = (
                jnp.where(row_id == 0, low_row, pltpu.roll(rise, 1, 0))
                + jnp.where(row_id == rows - 1, high_row, pltpu.roll(rise, rows - 1, 0))
                + jnp.where(lane_id == 0, rise, pltpu.roll(rise, 1, 1))
                + jnp.where(lane_id == columns - 1, rise, pltpu.roll(rise, columns - 1, 1))
                - 4.0 * rise
            )
            where = place[layer]
            surface = kinetic_ref[where]
            current = kinetic_ref[where + slots]
            kelvin = BASE_KELVIN + rise
            inverse_kelvin = 1.0 / kelvin
            base_rate = (
                RATE_CONSTANT
                * jnp.exp((RATE_ACTIVATION / BASE_KELVIN) * rise * inverse_kelvin)
                * jnp.sqrt(surface * (1.0 - surface))
            )
            ratio_rate = current / (2.0 * base_rate)
            arcsine, rooted = inverse_sine(ratio_rate)
            entropic = ENTROPY_SLOPE * (0.5 - surface)
            drive = VOLT_PER_KELVIN * arcsine + entropic
            scaled = HEAT_SCALE * current
            source = scaled * (kelvin * drive)
            slope = scaled * (
                drive - (VOLT_PER_KELVIN * RATE_ACTIVATION) * ratio_rate * inverse_kelvin / rooted
            )
            right = rise + INPLANE_CONDUCT * laplace + source - slope * rise
            if layer == 0 or layer == last:
                side = 0 if layer == 0 else 1
                partner = contacts_ref[side, cell]
                face = faces_ref[jnp.maximum(partner, 0)]
                face = jnp.where(partner >= 0, face, 0.0)
                right = right + CONTACT_CONDUCT * (face - rise)
            slope_ref[layer] = slope
            right_ref[layer] = right
        upper = value = None
        for layer in range(layers):
            diagonal = 1.0 - slope_ref[layer]
            source = right_ref[layer]
            if layer > 0:
                diagonal = diagonal + THROUGH_CONDUCT - THROUGH_CONDUCT * upper
                source = source + THROUGH_CONDUCT * value
            if layer < last:
                diagonal = diagonal + THROUGH_CONDUCT
            inverse = 1.0 / diagonal
            upper = THROUGH_CONDUCT * inverse
            value = source * inverse
            slope_ref[layer] = upper
            right_ref[layer] = value
        out_ref[last] = value
        for layer in range(last - 1, -1, -1):
            value = right_ref[layer] + slope_ref[layer] * value
            out_ref[layer] = value

    return pl.pallas_call(
        kernel,
        name="column",
        out_shape=jax.ShapeDtypeStruct(heat_rise.shape, jnp.float32),
        in_specs=[pl.BlockSpec(memory_space=SMEM)] * 2
        + [pl.BlockSpec(memory_space=HBM)]
        + [pl.BlockSpec(memory_space=VMEM)] * (4 + len(hops)),
        out_specs=pl.BlockSpec(memory_space=VMEM),
        scratch_shapes=[
            pltpu.SMEM((layers + slots,), jnp.int32),
            pltpu.VMEM((2 * blocks, rows, columns), jnp.float32),
            pltpu.VMEM((layers, rows, columns), jnp.float32),
            pltpu.VMEM((layers, rows, columns), jnp.float32),
        ],
        compiler_params=params(8),
        cost_estimate=pl.CostEstimate(
            flops=200 * layers * rows * columns, bytes_accessed=8 * layers * rows * columns, transcendentals=0
        ),
    )(layer_counts, contacts, *far(after), *near(heat_rise, mine, got, faces, *arrived))


def per_device(shell_conc, heat_rise, layer_current, layer_counts, contacts):
    shell_conc, heat_rise, layer_current = shell_conc[0], heat_rise[0], layer_current[0]
    slots = shell_conc.shape[0]
    layers, part, columns = heat_rise.shape
    devices = lax.axis_size("sub")
    chips = devices // 2
    hops = (1, -1, 2, -2, 3, -3, 4)
    contacts = contacts.T
    mine, theirs = split_kinetic(shell_conc, layer_current, heat_rise, chips)
    theirs, heat_behind = lax.optimization_barrier((theirs, heat_rise))
    send_rise, send_faces = pack_rise(heat_behind, layer_counts, contacts, slots)
    got_rise = lax.all_to_all(send_rise, "sub", 0, 0)
    got = lax.ppermute(theirs, "sub", [(i, i ^ 1) for i in range(devices)])
    arrived = [
        lax.ppermute(message, "sub", [(i, (i + 2 * hop) % devices) for i in range(devices)])
        for hop, message in zip(hops, pack_kinetic(mine, got, hops))
    ]
    got_rise, send_faces = lax.optimization_barrier((got_rise, send_faces))
    faces = lax.all_to_all(send_faces, "cell", 0, 0, tiled=True)
    conc_new = particle(shell_conc, got_rise, layer_current, layer_counts)
    heat_new = column(heat_rise, mine, got, arrived, hops, faces, conc_new, layer_counts, contacts)
    return conc_new[None], heat_new[None]


def solution(mesh):
    in_specs = (
        P("cell", "sub", None, None, None),
        P("cell", None, "sub", None),
        P("cell", "sub", None, None),
        P(),
        P(),
    )
    out_specs = (P("cell", "sub", None, None, None), P("cell", None, "sub", None))
    return jax.shard_map(
        per_device, mesh=mesh, in_specs=in_specs, out_specs=out_specs, check_vma=False
    )
```

```python
import functools

import jax
import jax.numpy as jnp
from jax import lax
from jax.experimental import pallas as pl
from jax.experimental.pallas import tpu as pltpu
from jax.sharding import PartitionSpec as P

BASE_KELVIN = 298.15
RATE_ACTIVATION = 5000.0
DIFFUSION_ACTIVATION = 3000.0
RATE_CONSTANT = 0.5
VOLT_PER_KELVIN = 2.0 * 8.314462618 / 96485.33212
HEAT_SCALE = 10.0
ENTROPY_SLOPE = 0.001
DIFFUSION_STEP = 0.005
SURFACE_STEP = 0.005
INPLANE_CONDUCT = 0.25
THROUGH_CONDUCT = 2.0
CONTACT_CONDUCT = 0.5

SMEM = pltpu.MemorySpace.SMEM
VMEM = pltpu.MemorySpace.VMEM
HBM = pltpu.MemorySpace.HBM


def reciprocal(value):
    return pl.reciprocal(value, approx=True)


def near(*arrays):
    return [pltpu.with_memory_space_constraint(array, VMEM) for array in arrays]


def far(*arrays):
    return [pltpu.with_memory_space_constraint(array, HBM) for array in arrays]


def params(mebibytes):
    return pltpu.CompilerParams(vmem_limit_bytes=mebibytes * 2**20)


def starts_of(counts_ref, devices):
    starts = [jnp.int32(0)]
    for d in range(devices):
        starts.append(starts[-1] + counts_ref[d])
    return starts


def along(hop, chips):
    return [
        pair
        for z in range(chips)
        for pair in ((2 * z, 2 * ((z + hop) % chips)), (2 * z + 1, 2 * ((z - hop) % chips) + 1))
    ]


def place_of():
    position = lax.axis_index("sub")
    core = position % 2
    return position, position // 2, core, 1 - 2 * core


def pair_counts(counts_ref, chip):
    return counts_ref[2 * chip], counts_ref[2 * chip + 1]


def split_kinetic(shell_conc, layer_current, chips):
    slots, shells, rows, columns = shell_conc.shape
    pair = rows // chips
    part = pair // 2
    hops = chips // 2

    def kernel(shell_ref, current_ref, mine_ref, theirs_ref, sem):
        position, chip, core, sign = place_of()
        copies = []
        for turn, target in enumerate((theirs_ref, mine_ref)):
            way = -sign if turn == 0 else sign
            side = 1 - core if turn == 0 else core
            for array, source in enumerate((shell_ref.at[:, shells - 1], current_ref)):
                for hop in range(1, hops):
                    to = lax.rem(chip + way * hop + chips, chips)
                    here = pl.ds(pl.multiple_of(to * pair, pair), pair)
                    there = target.at[pl.ds(((hop - 1) * 2 + array) * slots, slots)]
                    copies.append((source.at[:, here], there))
                for half, to in enumerate((chip, lax.rem(chip + hops, chips))):
                    here = pl.ds(pl.multiple_of(to * pair + side * part, part), part)
                    there = target.at[
                        pl.ds(((hops - 1) * 2 + array) * slots, slots), pl.ds(half * part, part)
                    ]
                    copies.append((source.at[:, here], there))
        copies = [pltpu.make_async_copy(*copy, sem.at[i]) for i, copy in enumerate(copies)]
        for copy in copies:
            copy.start()
        for copy in copies:
            copy.wait()

    return pl.pallas_call(
        kernel,
        name="split_kinetic",
        out_shape=(VMEM((hops * 2 * slots, pair, columns), jnp.float32),) * 2,
        compiler_params=params(4),
        in_specs=[pl.BlockSpec(memory_space=HBM)] * 2,
        out_specs=[pl.BlockSpec(memory_space=VMEM)] * 2,
        scratch_shapes=[pltpu.SemaphoreType.DMA((4 * (hops + 1),))],
    )(*far(shell_conc, layer_current))


def pack_rise(heat_rise, other_rise, layer_counts, contacts, room):
    layers, part, columns = heat_rise.shape
    devices = layer_counts.shape[0]
    chips, cells = devices // 2, contacts.shape[1]
    hops = chips // 2

    def kernel(counts_ref, contacts_ref, heat_ref, other_ref, *refs):
        send_refs, (faces_ref, table) = refs[:hops], refs[hops:]
        position, chip, core, sign = place_of()
        cell = lax.axis_index("cell")
        starts = starts_of(counts_ref, devices)
        for to in range(chips):
            table[to] = starts[2 * to]
        ours = pl.ds(pl.multiple_of(core * part, part), part)
        others = pl.ds(pl.multiple_of((1 - core) * part, part), part)
        for hop, send_ref in zip(range(1, hops + 1), send_refs):
            start = table[lax.rem(chip + sign * hop + chips, chips)]
            for j in range(room):
                layer = jnp.minimum(start + j, layers - 1)
                if hop < hops:
                    send_ref[j, ours] = heat_ref[layer]
                    send_ref[j, others] = other_ref[layer]
                else:
                    send_ref[j] = heat_ref[layer]
        for layer in range(layers):
            send_refs[0][room, layer : layer + 1] = jnp.where(
                core == 0, other_ref[layer, part - 1 : part], other_ref[layer, 0:1]
            )
        for j in range(cells):
            faces_ref[j] = heat_ref[jnp.where(contacts_ref[0, j] == cell, layers - 1, 0)]

    return pl.pallas_call(
        kernel,
        name="pack_rise",
        out_shape=(
            VMEM((room + 1, 2 * part, columns), jnp.float32),
            *[VMEM((room, 2 * part, columns), jnp.float32)] * (hops - 2),
            VMEM((room, part, columns), jnp.float32),
            VMEM((cells, part, columns), jnp.float32),
        ),
        compiler_params=params(4),
        in_specs=[pl.BlockSpec(memory_space=SMEM)] * 2 + [pl.BlockSpec(memory_space=VMEM)] * 2,
        out_specs=[pl.BlockSpec(memory_space=VMEM)] * (hops + 1),
        scratch_shapes=[pltpu.SMEM((chips,), jnp.int32)],
    )(layer_counts, contacts, *near(heat_rise, other_rise))


def pack_kinetic(mine, got, layer_counts, room):
    blocks, pair, columns = mine.shape
    hops = layer_counts.shape[0] // 4
    slots = blocks // (2 * hops)
    part = pair // 2

    def kernel(counts_ref, mine_ref, got_ref, *refs):
        send_refs, (home_ref, both) = refs[:hops], refs[hops:]
        position, chip, core, sign = place_of()
        both[core] = mine_ref[...]
        both[1 - core] = got_ref[...]
        first, second = pair_counts(counts_ref, chip)
        for j in range(room):
            side = jnp.where(j < first, 0, 1)
            slot = jnp.minimum(j - side * first, slots - 1)
            for array in range(2):
                for hop in range(1, hops):
                    send_refs[hop - 1][array * room + j] = both[side, ((hop - 1) * 2 + array) * slots + slot]
                block = ((hops - 1) * 2 + array) * slots + slot
                home_ref[array * room + j] = both[side, block, 0:part]
                send_refs[hops - 1][array * room + j] = both[side, block, part:pair]

    return pl.pallas_call(
        kernel,
        name="pack_kinetic",
        out_shape=(
            *[VMEM((2 * room, pair, columns), jnp.float32)] * (hops - 1),
            *[VMEM((2 * room, part, columns), jnp.float32)] * 2,
        ),
        compiler_params=params(4),
        in_specs=[pl.BlockSpec(memory_space=SMEM)] + [pl.BlockSpec(memory_space=VMEM)] * 2,
        out_specs=[pl.BlockSpec(memory_space=VMEM)] * (hops + 1),
        scratch_shapes=[pltpu.VMEM((2, blocks, pair, columns), jnp.float32)],
    )(layer_counts, *near(mine, got))


def pass_rise(arrived, layer_counts, slots, room):
    _, pair, columns = arrived[0].shape
    hops = len(arrived)
    part = pair // 2

    def kernel(counts_ref, *refs):
        arrived_refs, pass_ref = refs[:hops], refs[hops]
        position, chip, core, sign = place_of()
        base = jnp.where(core == 1, 0, counts_ref[2 * chip])
        for s in range(slots):
            j = jnp.minimum(base + s, room - 1)
            for hop in range(1, hops):
                pass_ref[(hop - 1) * slots + s] = arrived_refs[hop - 1][j]
            half = s % 2 * part
            pass_ref[(hops - 1) * slots + s // 2, half : half + part] = arrived_refs[hops - 1][j]

    return pl.pallas_call(
        kernel,
        name="pass_rise",
        out_shape=VMEM(((hops - 1) * slots + slots // 2, pair, columns), jnp.float32),
        compiler_params=params(4),
        in_specs=[pl.BlockSpec(memory_space=SMEM)] + [pl.BlockSpec(memory_space=VMEM)] * hops,
        out_specs=pl.BlockSpec(memory_space=VMEM),
    )(layer_counts, *near(*arrived))


def pass_kinetic(arrived, after):
    each, pair, columns = arrived[0].shape
    part = pair // 2

    def kernel(_, *refs):
        others = pl.ds(pl.multiple_of((1 - place_of()[2]) * part, part), part)
        for i, ref in enumerate(refs[:-1]):
            refs[-1][i * each : (i + 1) * each] = ref[:, others]

    return pl.pallas_call(
        kernel,
        name="pass_kinetic",
        out_shape=VMEM((len(arrived) * each, part, columns), jnp.float32),
        compiler_params=params(4),
        in_specs=[pl.BlockSpec(memory_space=HBM)] + [pl.BlockSpec(memory_space=VMEM)] * len(arrived),
        out_specs=pl.BlockSpec(memory_space=VMEM),
    )(*far(after), *near(*arrived))


def particle(
    shell_conc, heat_rise, other_rise, arrived, passed, layer_current, layer_counts, pieces=2, chunk=64
):
    slots, shells, rows, columns = shell_conc.shape
    layers, part, _ = heat_rise.shape
    devices = layer_counts.shape[0]
    chips, hops, pair = devices // 2, len(arrived), 2 * part
    room = arrived[0].shape[0] - 1
    piece = rows // pieces
    volume = [((i + 1) ** 3 - i**3) / (3.0 * shells**3) for i in range(shells)]
    link = [DIFFUSION_STEP * ((i + 1) ** 2 / shells**2 * shells) for i in range(shells - 1)]

    def kernel(counts_ref, states_ref, current_ref, heat_ref, other_ref, passed_ref, *refs):
        arrived_refs, (out_ref, rise_ref, shell_ref, made, sem, got_sem) = refs[:hops], refs[hops:]
        fetches = [
            pltpu.make_async_copy(states_ref.at[slot], shell_ref.at[slot], got_sem.at[slot])
            for slot in range(slots)
        ]
        for fetch in fetches:
            fetch.start()
        position, chip, core, sign = place_of()
        count = counts_ref[position]
        start = lax.fori_loop(0, position, lambda d, total: total + counts_ref[d], jnp.int32(0))
        base = jnp.where(core == 0, 0, counts_ref[2 * chip])

        def rows_of(hop, begin, extent):
            first = lax.rem(chip + hop + chips, chips) * pair + begin
            return pl.ds(pl.multiple_of(first, part), extent)

        for s in range(slots):
            layer, j = jnp.minimum(start + s, layers - 1), jnp.minimum(base + s, room - 1)
            rise_ref[s, rows_of(0, core * part, part)] = heat_ref[layer]
            rise_ref[s, rows_of(0, (1 - core) * part, part)] = other_ref[layer]
            for hop in range(1, hops):
                rise_ref[s, rows_of(-sign * hop, 0, pair)] = arrived_refs[hop - 1][j]
                rise_ref[s, rows_of(sign * hop, 0, pair)] = passed_ref[(hop - 1) * slots + s]
            half = s % 2 * part
            rise_ref[s, rows_of(hops, core * part, part)] = arrived_refs[hops - 1][j]
            rise_ref[s, rows_of(hops, (1 - core) * part, part)] = passed_ref[
                (hops - 1) * slots + s // 2, half : half + part
            ]

        def solve(slot, first):
            here = slice(first, first + chunk)
            rise = rise_ref[slot, here]
            scaled = rise * (DIFFUSION_ACTIVATION / BASE_KELVIN)
            speedup = jnp.exp(scaled * reciprocal(BASE_KELVIN + rise))
            held = [None] * shells
            inverse = [None] * shells
            capacity = amount = upper = None
            for i in range(shells):
                gain = volume[i] * shell_ref[slot, i, here]
                if i == 0:
                    capacity, amount = volume[0], gain
                else:
                    capacity = volume[i] + upper * capacity
                    amount = gain + upper * amount
                if i < shells - 1:
                    flow = link[i] * speedup
                    inverse[i] = reciprocal(capacity + flow)
                    upper = flow * inverse[i]
                else:
                    amount = amount - SURFACE_STEP * current_ref[slot, here]
                    inverse[i] = reciprocal(capacity)
                held[i] = amount
            value = held[-1] * inverse[-1]
            made[slot, shells - 1, here] = value
            for i in range(shells - 2, -1, -1):
                value = inverse[i] * (held[i] + (link[i] * speedup) * value)
                made[slot, i, here] = value

        copies = []
        for slot in range(slots):
            fetches[slot].wait()
            for first in range(0, rows, piece):
                here = slice(first, first + piece)

                @pl.when(slot < count)
                def _(slot=slot, first=first):
                    for begin in range(first, first + piece, chunk):
                        solve(slot, begin)

                @pl.when(slot >= count)
                def _(slot=slot, here=here):
                    made[slot, :, here] = jnp.zeros((shells, piece, columns), jnp.float32)

                copies.append(
                    pltpu.make_async_copy(made.at[slot, :, here], out_ref.at[slot, :, here], sem.at[len(copies)])
                )
                copies[-1].start()
        for copy in copies:
            copy.wait()

    return pl.pallas_call(
        kernel,
        name="particle",
        out_shape=HBM(shell_conc.shape, jnp.float32),
        in_specs=[pl.BlockSpec(memory_space=SMEM), pl.BlockSpec(memory_space=HBM)]
        + [pl.BlockSpec(memory_space=VMEM)] * (4 + hops),
        out_specs=pl.BlockSpec(memory_space=HBM),
        scratch_shapes=[
            pltpu.VMEM((slots, rows, columns), jnp.float32),
            pltpu.VMEM(shell_conc.shape, jnp.float32),
            pltpu.VMEM(shell_conc.shape, jnp.float32),
            pltpu.SemaphoreType.DMA((slots * pieces,)),
            pltpu.SemaphoreType.DMA((slots,)),
        ],
        compiler_params=params(16),
        cost_estimate=pl.CostEstimate(
            flops=200 * slots * shells * rows * columns,
            bytes_accessed=8 * slots * shells * rows * columns,
            transcendentals=0,
        ),
    )(layer_counts, *far(shell_conc), *near(layer_current, heat_rise, other_rise, passed, *arrived))


def inverse_sine(value):
    magnitude = jnp.abs(value)
    rooted = jnp.sqrt(1.0 + magnitude * magnitude)
    positive = jnp.log1p(magnitude + magnitude * magnitude / (1.0 + rooted))
    return jnp.where(value < 0.0, -positive, positive), rooted


def column(heat_rise, other_rise, rise_edge, home, passed, arrived, faces, layer_counts, contacts):
    layers, rows, columns = heat_rise.shape
    devices = layer_counts.shape[0]
    chips, hops = devices // 2, len(arrived)
    each = home.shape[0]
    room = each // 2
    edge = rise_edge.shape[0] - 1
    last = layers - 1

    def kernel(counts_ref, contacts_ref, heat_ref, other_ref, edge_ref, faces_ref, home_ref, passed_ref, *refs):
        arrived_refs, (out_ref, place, kinetic_ref, slope_ref, right_ref) = refs[:hops], refs[hops:]
        position, chip, core, sign = place_of()
        cell = lax.axis_index("cell")
        ours = pl.ds(pl.multiple_of(core * rows, rows), rows)
        kinetic_ref[0:each] = home_ref[...]
        for hop in range(1, hops):
            kinetic_ref[hop * each : (hop + 1) * each] = arrived_refs[hop - 1][:, ours]
            back = chips - hop
            kinetic_ref[back * each : (back + 1) * each] = passed_ref[(hop - 1) * each : hop * each]
        kinetic_ref[hops * each : (hops + 1) * each] = arrived_refs[hops - 1][...]
        starts = starts_of(counts_ref, devices)
        for owner in range(chips):
            hop = lax.rem(sign * (chip - owner) + chips, chips)
            for j in range(room):
                place[starts[2 * owner] + j] = hop * each + j
        row_id = lax.broadcasted_iota(jnp.int32, (rows, columns), 0)
        lane_id = lax.broadcasted_iota(jnp.int32, (rows, columns), 1)
        for layer in range(layers):
            rise = heat_ref[layer]
            beyond = edge_ref[edge, layer : layer + 1]
            low_row = jnp.where(core == 0, beyond, other_ref[layer, rows - 1 : rows])
            high_row = jnp.where(core == 0, other_ref[layer, 0:1], beyond)
            low_row = jnp.where(position == 0, rise[0:1], low_row)
            high_row = jnp.where(position == devices - 1, rise[rows - 1 : rows], high_row)
            laplace = (
                jnp.where(row_id == 0, low_row, pltpu.roll(rise, 1, 0))
                + jnp.where(row_id == rows - 1, high_row, pltpu.roll(rise, rows - 1, 0))
                + jnp.where(lane_id == 0, rise, pltpu.roll(rise, 1, 1))
                + jnp.where(lane_id == columns - 1, rise, pltpu.roll(rise, columns - 1, 1))
                - 4.0 * rise
            )
            where = place[layer]
            surface = kinetic_ref[where]
            current = kinetic_ref[where + room]
            kelvin = BASE_KELVIN + rise
            inverse_kelvin = 1.0 / kelvin
            base_rate = (
                RATE_CONSTANT
                * jnp.exp((RATE_ACTIVATION / BASE_KELVIN) * rise * inverse_kelvin)
                * jnp.sqrt(surface * (1.0 - surface))
            )
            ratio_rate = current / (2.0 * base_rate)
            arcsine, rooted = inverse_sine(ratio_rate)
            entropic = ENTROPY_SLOPE * (0.5 - surface)
            drive = VOLT_PER_KELVIN * arcsine + entropic
            scaled = HEAT_SCALE * current
            source = scaled * (kelvin * drive)
            slope = scaled * (
                drive - (VOLT_PER_KELVIN * RATE_ACTIVATION) * ratio_rate * inverse_kelvin / rooted
            )
            right = rise + INPLANE_CONDUCT * laplace + source - slope * rise
            if layer == 0 or layer == last:
                side = 0 if layer == 0 else 1
                partner = contacts_ref[side, cell]
                face = faces_ref[jnp.maximum(partner, 0)]
                face = jnp.where(partner >= 0, face, 0.0)
                right = right + CONTACT_CONDUCT * (face - rise)
            slope_ref[layer] = slope
            right_ref[layer] = right
        upper = value = None
        for layer in range(layers):
            diagonal = 1.0 - slope_ref[layer]
            source = right_ref[layer]
            if layer > 0:
                diagonal = diagonal + THROUGH_CONDUCT - THROUGH_CONDUCT * upper
                source = source + THROUGH_CONDUCT * value
            if layer < last:
                diagonal = diagonal + THROUGH_CONDUCT
            inverse = 1.0 / diagonal
            upper = THROUGH_CONDUCT * inverse
            value = source * inverse
            slope_ref[layer] = upper
            right_ref[layer] = value
        out_ref[last] = value
        for layer in range(last - 1, -1, -1):
            value = right_ref[layer] + slope_ref[layer] * value
            out_ref[layer] = value

    return pl.pallas_call(
        kernel,
        name="column",
        out_shape=jax.ShapeDtypeStruct(heat_rise.shape, jnp.float32),
        in_specs=[pl.BlockSpec(memory_space=SMEM)] * 2 + [pl.BlockSpec(memory_space=VMEM)] * (6 + hops),
        out_specs=pl.BlockSpec(memory_space=VMEM),
        scratch_shapes=[
            pltpu.SMEM((layers + room,), jnp.int32),
            pltpu.VMEM((chips * each, rows, columns), jnp.float32),
            pltpu.VMEM((layers, rows, columns), jnp.float32),
            pltpu.VMEM((layers, rows, columns), jnp.float32),
        ],
        compiler_params=params(8),
        cost_estimate=pl.CostEstimate(
            flops=200 * layers * rows * columns, bytes_accessed=8 * layers * rows * columns, transcendentals=0
        ),
    )(layer_counts, contacts, *near(heat_rise, other_rise, rise_edge, faces, home, passed, *arrived))


def per_device(shell_conc, heat_rise, layer_current, layer_counts, contacts):
    shell_conc, heat_rise, layer_current = shell_conc[0], heat_rise[0], layer_current[0]
    slots = shell_conc.shape[0]
    layers, part, columns = heat_rise.shape
    devices = lax.axis_size("sub")
    chips = devices // 2
    room = 2 * slots
    contacts = contacts.T
    swap = [(i, i ^ 1) for i in range(devices)]
    other_rise = lax.ppermute(heat_rise, "sub", swap)
    mine, theirs = split_kinetic(shell_conc, layer_current, chips)
    got = lax.ppermute(theirs, "sub", swap)
    *send_rise, send_faces = pack_rise(heat_rise, other_rise, layer_counts, contacts, room)
    *send_kinetic, home = pack_kinetic(mine, got, layer_counts, room)
    send_rise[2:], send_kinetic = lax.optimization_barrier((send_rise[2:], send_kinetic))
    rise = [lax.ppermute(m, "sub", along(hop, chips)) for hop, m in enumerate(send_rise, 1)]
    for i, j in ((0, 2), (1, 1), (2, 0)):
        rise[i], send_kinetic[j] = lax.optimization_barrier((rise[i], send_kinetic[j]))
    kinetic = [lax.ppermute(m, "sub", along(hop, chips)) for hop, m in enumerate(send_kinetic, 1)]
    rise[3], send_faces = lax.optimization_barrier((rise[3], send_faces))
    faces = lax.all_to_all(send_faces, "cell", 0, 0, tiled=True)
    passed_rise = lax.ppermute(pass_rise(rise, layer_counts, slots, room), "sub", swap)
    conc_new = particle(shell_conc, heat_rise, other_rise, rise, passed_rise, layer_current, layer_counts)
    kinetic, faces = lax.optimization_barrier((kinetic, faces))
    passed_kinetic = lax.ppermute(pass_kinetic(kinetic[:-1], conc_new), "sub", swap)
    heat_new = column(
        heat_rise, other_rise, rise[0], home, passed_kinetic, kinetic, faces, layer_counts, contacts
    )
    return conc_new[None], heat_new[None]


def solution(mesh):
    in_specs = (
        P("cell", "sub", None, None, None),
        P("cell", None, "sub", None),
        P("cell", "sub", None, None),
        P(),
        P(),
    )
    out_specs = (P("cell", "sub", None, None, None), P("cell", None, "sub", None))
    return jax.shard_map(
        per_device, mesh=mesh, in_specs=in_specs, out_specs=out_specs, check_vma=False
    )
```

```python
import functools

import jax
import jax.numpy as jnp
from jax import lax
from jax.experimental import pallas as pl
from jax.experimental.pallas import tpu as pltpu
from jax.sharding import PartitionSpec as P

BASE_KELVIN = 298.15
RATE_ACTIVATION = 5000.0
DIFFUSION_ACTIVATION = 3000.0
RATE_CONSTANT = 0.5
VOLT_PER_KELVIN = 2.0 * 8.314462618 / 96485.33212
HEAT_SCALE = 10.0
ENTROPY_SLOPE = 0.001
DIFFUSION_STEP = 0.005
SURFACE_STEP = 0.005
INPLANE_CONDUCT = 0.25
THROUGH_CONDUCT = 2.0
CONTACT_CONDUCT = 0.5

SMEM = pltpu.MemorySpace.SMEM
VMEM = pltpu.MemorySpace.VMEM
HBM = pltpu.MemorySpace.HBM


def reciprocal(value):
    return pl.reciprocal(value, approx=True)


def near(*arrays):
    return [pltpu.with_memory_space_constraint(array, VMEM) for array in arrays]


def far(*arrays):
    return [pltpu.with_memory_space_constraint(array, HBM) for array in arrays]


def params(mebibytes):
    return pltpu.CompilerParams(vmem_limit_bytes=mebibytes * 2**20)


def starts_of(counts_ref, devices):
    starts = [jnp.int32(0)]
    for d in range(devices):
        starts.append(starts[-1] + counts_ref[d])
    return starts


def along(hop, chips):
    return [
        pair
        for z in range(chips)
        for pair in ((2 * z, 2 * ((z + hop) % chips)), (2 * z + 1, 2 * ((z - hop) % chips) + 1))
    ]


def place_of():
    position = lax.axis_index("sub")
    core = position % 2
    return position, position // 2, core, 1 - 2 * core


def pair_counts(counts_ref, chip):
    return counts_ref[2 * chip], counts_ref[2 * chip + 1]


def split_kinetic(shell_conc, layer_current, chips):
    slots, shells, rows, columns = shell_conc.shape
    pair = rows // chips
    part = pair // 2
    hops = chips // 2

    def kernel(shell_ref, current_ref, mine_ref, theirs_ref, sem):
        position, chip, core, sign = place_of()
        copies = []
        for turn, target in enumerate((theirs_ref, mine_ref)):
            way = -sign if turn == 0 else sign
            side = 1 - core if turn == 0 else core
            for array, source in enumerate((shell_ref.at[:, shells - 1], current_ref)):
                for hop in range(1, hops):
                    to = lax.rem(chip + way * hop + chips, chips)
                    here = pl.ds(pl.multiple_of(to * pair, pair), pair)
                    there = target.at[pl.ds(((hop - 1) * 2 + array) * slots, slots)]
                    copies.append((source.at[:, here], there))
                for half, to in enumerate((chip, lax.rem(chip + hops, chips))):
                    here = pl.ds(pl.multiple_of(to * pair + side * part, part), part)
                    there = target.at[
                        pl.ds(((hops - 1) * 2 + array) * slots, slots), pl.ds(half * part, part)
                    ]
                    copies.append((source.at[:, here], there))
        copies = [pltpu.make_async_copy(*copy, sem.at[i]) for i, copy in enumerate(copies)]
        for copy in copies:
            copy.start()
        for copy in copies:
            copy.wait()

    return pl.pallas_call(
        kernel,
        name="split_kinetic",
        out_shape=(VMEM((hops * 2 * slots, pair, columns), jnp.float32),) * 2,
        compiler_params=params(4),
        in_specs=[pl.BlockSpec(memory_space=HBM)] * 2,
        out_specs=[pl.BlockSpec(memory_space=VMEM)] * 2,
        scratch_shapes=[pltpu.SemaphoreType.DMA((4 * (hops + 1),))],
    )(*far(shell_conc, layer_current))


def pack_rise(heat_rise, other_rise, layer_counts, contacts, room):
    layers, part, columns = heat_rise.shape
    devices = layer_counts.shape[0]
    chips, cells = devices // 2, contacts.shape[1]
    hops = chips // 2

    def kernel(counts_ref, contacts_ref, heat_ref, other_ref, *refs):
        send_refs, (faces_ref, table) = refs[:hops], refs[hops:]
        position, chip, core, sign = place_of()
        cell = lax.axis_index("cell")
        starts = starts_of(counts_ref, devices)
        for to in range(chips):
            table[to] = starts[2 * to]
        ours = pl.ds(pl.multiple_of(core * part, part), part)
        others = pl.ds(pl.multiple_of((1 - core) * part, part), part)
        for hop, send_ref in zip(range(1, hops + 1), send_refs):
            start = table[lax.rem(chip + sign * hop + chips, chips)]
            for j in range(room):
                layer = jnp.minimum(start + j, layers - 1)
                if hop < hops:
                    send_ref[j, ours] = heat_ref[layer]
                    send_ref[j, others] = other_ref[layer]
                else:
                    send_ref[j] = heat_ref[layer]
        for layer in range(layers):
            send_refs[0][room, layer : layer + 1] = jnp.where(
                core == 0, other_ref[layer, part - 1 : part], other_ref[layer, 0:1]
            )
        for j in range(cells):
            faces_ref[j] = heat_ref[jnp.where(contacts_ref[0, j] == cell, layers - 1, 0)]

    return pl.pallas_call(
        kernel,
        name="pack_rise",
        out_shape=(
            VMEM((room + 1, 2 * part, columns), jnp.float32),
            *[VMEM((room, 2 * part, columns), jnp.float32)] * (hops - 2),
            VMEM((room, part, columns), jnp.float32),
            VMEM((cells, part, columns), jnp.float32),
        ),
        compiler_params=params(4),
        in_specs=[pl.BlockSpec(memory_space=SMEM)] * 2 + [pl.BlockSpec(memory_space=VMEM)] * 2,
        out_specs=[pl.BlockSpec(memory_space=VMEM)] * (hops + 1),
        scratch_shapes=[pltpu.SMEM((chips,), jnp.int32)],
    )(layer_counts, contacts, *near(heat_rise, other_rise))


def pack_kinetic(mine, got, layer_counts, room):
    blocks, pair, columns = mine.shape
    hops = layer_counts.shape[0] // 4
    slots = blocks // (2 * hops)
    part = pair // 2

    def kernel(counts_ref, mine_ref, got_ref, *refs):
        send_refs, (home_ref, both) = refs[:hops], refs[hops:]
        position, chip, core, sign = place_of()
        both[core] = mine_ref[...]
        both[1 - core] = got_ref[...]
        first, second = pair_counts(counts_ref, chip)
        for j in range(room):
            side = jnp.where(j < first, 0, 1)
            slot = jnp.minimum(j - side * first, slots - 1)
            for array in range(2):
                for hop in range(1, hops):
                    send_refs[hop - 1][array * room + j] = both[side, ((hop - 1) * 2 + array) * slots + slot]
                block = ((hops - 1) * 2 + array) * slots + slot
                home_ref[array * room + j] = both[side, block, 0:part]
                send_refs[hops - 1][array * room + j] = both[side, block, part:pair]

    return pl.pallas_call(
        kernel,
        name="pack_kinetic",
        out_shape=(
            *[VMEM((2 * room, pair, columns), jnp.float32)] * (hops - 1),
            *[VMEM((2 * room, part, columns), jnp.float32)] * 2,
        ),
        compiler_params=params(4),
        in_specs=[pl.BlockSpec(memory_space=SMEM)] + [pl.BlockSpec(memory_space=VMEM)] * 2,
        out_specs=[pl.BlockSpec(memory_space=VMEM)] * (hops + 1),
        scratch_shapes=[pltpu.VMEM((2, blocks, pair, columns), jnp.float32)],
    )(layer_counts, *near(mine, got))


def pass_rise(arrived, layer_counts, slots, room):
    _, pair, columns = arrived[0].shape
    hops = len(arrived)
    part = pair // 2

    def kernel(counts_ref, *refs):
        arrived_refs, pass_ref = refs[:hops], refs[hops]
        position, chip, core, sign = place_of()
        base = jnp.where(core == 1, 0, counts_ref[2 * chip])
        for s in range(slots):
            j = jnp.minimum(base + s, room - 1)
            for hop in range(1, hops):
                pass_ref[(hop - 1) * slots + s] = arrived_refs[hop - 1][j]
            half = s % 2 * part
            pass_ref[(hops - 1) * slots + s // 2, half : half + part] = arrived_refs[hops - 1][j]

    return pl.pallas_call(
        kernel,
        name="pass_rise",
        out_shape=VMEM(((hops - 1) * slots + slots // 2, pair, columns), jnp.float32),
        compiler_params=params(4),
        in_specs=[pl.BlockSpec(memory_space=SMEM)] + [pl.BlockSpec(memory_space=VMEM)] * hops,
        out_specs=pl.BlockSpec(memory_space=VMEM),
    )(layer_counts, *near(*arrived))


def pass_kinetic(arrived, after):
    each, pair, columns = arrived[0].shape
    part = pair // 2

    def kernel(_, *refs):
        others = pl.ds(pl.multiple_of((1 - place_of()[2]) * part, part), part)
        for i, ref in enumerate(refs[:-1]):
            refs[-1][i * each : (i + 1) * each] = ref[:, others]

    return pl.pallas_call(
        kernel,
        name="pass_kinetic",
        out_shape=VMEM((len(arrived) * each, part, columns), jnp.float32),
        compiler_params=params(4),
        in_specs=[pl.BlockSpec(memory_space=HBM)] + [pl.BlockSpec(memory_space=VMEM)] * len(arrived),
        out_specs=pl.BlockSpec(memory_space=VMEM),
    )(*far(after), *near(*arrived))


def particle(
    shell_conc, heat_rise, other_rise, arrived, passed, layer_current, layer_counts, pieces=2, chunk=64
):
    slots, shells, rows, columns = shell_conc.shape
    layers, part, _ = heat_rise.shape
    devices = layer_counts.shape[0]
    chips, hops, pair = devices // 2, len(arrived), 2 * part
    room = arrived[0].shape[0] - 1
    piece = rows // pieces
    volume = [((i + 1) ** 3 - i**3) / (3.0 * shells**3) for i in range(shells)]
    link = [DIFFUSION_STEP * ((i + 1) ** 2 / shells**2 * shells) for i in range(shells - 1)]

    def kernel(counts_ref, states_ref, current_ref, heat_ref, other_ref, passed_ref, *refs):
        arrived_refs, (out_ref, rise_ref, shell_ref, made, sem, got_sem) = refs[:hops], refs[hops:]
        fetches = [
            pltpu.make_async_copy(states_ref.at[slot], shell_ref.at[slot], got_sem.at[slot])
            for slot in range(slots)
        ]
        for fetch in fetches:
            fetch.start()
        position, chip, core, sign = place_of()
        count = counts_ref[position]
        start = lax.fori_loop(0, position, lambda d, total: total + counts_ref[d], jnp.int32(0))
        base = jnp.where(core == 0, 0, counts_ref[2 * chip])

        def rows_of(hop, begin, extent):
            first = lax.rem(chip + hop + chips, chips) * pair + begin
            return pl.ds(pl.multiple_of(first, part), extent)

        for s in range(slots):
            layer, j = jnp.minimum(start + s, layers - 1), jnp.minimum(base + s, room - 1)
            rise_ref[s, rows_of(0, core * part, part)] = heat_ref[layer]
            rise_ref[s, rows_of(0, (1 - core) * part, part)] = other_ref[layer]
            for hop in range(1, hops):
                rise_ref[s, rows_of(-sign * hop, 0, pair)] = arrived_refs[hop - 1][j]
                rise_ref[s, rows_of(sign * hop, 0, pair)] = passed_ref[(hop - 1) * slots + s]
            half = s % 2 * part
            rise_ref[s, rows_of(hops, core * part, part)] = arrived_refs[hops - 1][j]
            rise_ref[s, rows_of(hops, (1 - core) * part, part)] = passed_ref[
                (hops - 1) * slots + s // 2, half : half + part
            ]

        def solve(slot, first):
            here = slice(first, first + chunk)
            rise = rise_ref[slot, here]
            scaled = rise * (DIFFUSION_ACTIVATION / BASE_KELVIN)
            speedup = jnp.exp(scaled * reciprocal(BASE_KELVIN + rise))
            held = [None] * shells
            inverse = [None] * shells
            capacity = amount = upper = None
            for i in range(shells):
                gain = volume[i] * shell_ref[slot, i, here]
                if i == 0:
                    capacity, amount = volume[0], gain
                else:
                    capacity = volume[i] + upper * capacity
                    amount = gain + upper * amount
                if i < shells - 1:
                    flow = link[i] * speedup
                    inverse[i] = reciprocal(capacity + flow)
                    upper = flow * inverse[i]
                else:
                    amount = amount - SURFACE_STEP * current_ref[slot, here]
                    inverse[i] = reciprocal(capacity)
                held[i] = amount
            value = held[-1] * inverse[-1]
            made[slot, shells - 1, here] = value
            for i in range(shells - 2, -1, -1):
                value = inverse[i] * (held[i] + (link[i] * speedup) * value)
                made[slot, i, here] = value

        copies = []
        for slot in range(slots):
            fetches[slot].wait()
            for first in range(0, rows, piece):
                here = slice(first, first + piece)

                @pl.when(slot < count)
                def _(slot=slot, first=first):
                    for begin in range(first, first + piece, chunk):
                        solve(slot, begin)

                @pl.when(slot >= count)
                def _(slot=slot, here=here):
                    made[slot, :, here] = jnp.zeros((shells, piece, columns), jnp.float32)

                copies.append(
                    pltpu.make_async_copy(made.at[slot, :, here], out_ref.at[slot, :, here], sem.at[len(copies)])
                )
                copies[-1].start()
        for copy in copies:
            copy.wait()

    return pl.pallas_call(
        kernel,
        name="particle",
        out_shape=HBM(shell_conc.shape, jnp.float32),
        in_specs=[pl.BlockSpec(memory_space=SMEM), pl.BlockSpec(memory_space=HBM)]
        + [pl.BlockSpec(memory_space=VMEM)] * (4 + hops),
        out_specs=pl.BlockSpec(memory_space=HBM),
        scratch_shapes=[
            pltpu.VMEM((slots, rows, columns), jnp.float32),
            pltpu.VMEM(shell_conc.shape, jnp.float32),
            pltpu.VMEM(shell_conc.shape, jnp.float32),
            pltpu.SemaphoreType.DMA((slots * pieces,)),
            pltpu.SemaphoreType.DMA((slots,)),
        ],
        compiler_params=params(16),
        cost_estimate=pl.CostEstimate(
            flops=200 * slots * shells * rows * columns,
            bytes_accessed=8 * slots * shells * rows * columns,
            transcendentals=0,
        ),
    )(layer_counts, *far(shell_conc), *near(layer_current, heat_rise, other_rise, passed, *arrived))


def inverse_sine(value):
    magnitude = jnp.abs(value)
    rooted = jnp.sqrt(1.0 + magnitude * magnitude)
    positive = jnp.log1p(magnitude + magnitude * magnitude / (1.0 + rooted))
    return jnp.where(value < 0.0, -positive, positive), rooted


def column(heat_rise, other_rise, rise_edge, home, passed, arrived, faces, layer_counts, contacts):
    layers, rows, columns = heat_rise.shape
    devices = layer_counts.shape[0]
    chips, hops = devices // 2, len(arrived)
    each = home.shape[0]
    room = each // 2
    edge = rise_edge.shape[0] - 1
    last = layers - 1

    def kernel(counts_ref, contacts_ref, heat_ref, other_ref, edge_ref, faces_ref, home_ref, passed_ref, *refs):
        arrived_refs, (out_ref, place, kinetic_ref, slope_ref, right_ref) = refs[:hops], refs[hops:]
        position, chip, core, sign = place_of()
        cell = lax.axis_index("cell")
        ours = pl.ds(pl.multiple_of(core * rows, rows), rows)
        kinetic_ref[0:each] = home_ref[...]
        for hop in range(1, hops):
            kinetic_ref[hop * each : (hop + 1) * each] = arrived_refs[hop - 1][:, ours]
            back = chips - hop
            kinetic_ref[back * each : (back + 1) * each] = passed_ref[(hop - 1) * each : hop * each]
        kinetic_ref[hops * each : (hops + 1) * each] = arrived_refs[hops - 1][...]
        starts = starts_of(counts_ref, devices)
        for owner in range(chips):
            hop = lax.rem(sign * (chip - owner) + chips, chips)
            for j in range(room):
                place[starts[2 * owner] + j] = hop * each + j
        row_id = lax.broadcasted_iota(jnp.int32, (rows, columns), 0)
        lane_id = lax.broadcasted_iota(jnp.int32, (rows, columns), 1)
        for layer in range(layers):
            rise = heat_ref[layer]
            beyond = edge_ref[edge, layer : layer + 1]
            low_row = jnp.where(core == 0, beyond, other_ref[layer, rows - 1 : rows])
            high_row = jnp.where(core == 0, other_ref[layer, 0:1], beyond)
            low_row = jnp.where(position == 0, rise[0:1], low_row)
            high_row = jnp.where(position == devices - 1, rise[rows - 1 : rows], high_row)
            laplace = (
                jnp.where(row_id == 0, low_row, pltpu.roll(rise, 1, 0))
                + jnp.where(row_id == rows - 1, high_row, pltpu.roll(rise, rows - 1, 0))
                + jnp.where(lane_id == 0, rise, pltpu.roll(rise, 1, 1))
                + jnp.where(lane_id == columns - 1, rise, pltpu.roll(rise, columns - 1, 1))
                - 4.0 * rise
            )
            where = place[layer]
            surface = kinetic_ref[where]
            current = kinetic_ref[where + room]
            kelvin = BASE_KELVIN + rise
            inverse_kelvin = 1.0 / kelvin
            base_rate = (
                RATE_CONSTANT
                * jnp.exp((RATE_ACTIVATION / BASE_KELVIN) * rise * inverse_kelvin)
                * jnp.sqrt(surface * (1.0 - surface))
            )
            ratio_rate = current / (2.0 * base_rate)
            arcsine, rooted = inverse_sine(ratio_rate)
            entropic = ENTROPY_SLOPE * (0.5 - surface)
            drive = VOLT_PER_KELVIN * arcsine + entropic
            scaled = HEAT_SCALE * current
            source = scaled * (kelvin * drive)
            slope = scaled * (
                drive - (VOLT_PER_KELVIN * RATE_ACTIVATION) * ratio_rate * inverse_kelvin / rooted
            )
            right = rise + INPLANE_CONDUCT * laplace + source - slope * rise
            if layer == 0 or layer == last:
                side = 0 if layer == 0 else 1
                partner = contacts_ref[side, cell]
                face = faces_ref[jnp.maximum(partner, 0)]
                face = jnp.where(partner >= 0, face, 0.0)
                right = right + CONTACT_CONDUCT * (face - rise)
            slope_ref[layer] = slope
            right_ref[layer] = right
        upper = value = None
        for layer in range(layers):
            diagonal = 1.0 - slope_ref[layer]
            source = right_ref[layer]
            if layer > 0:
                diagonal = diagonal + THROUGH_CONDUCT - THROUGH_CONDUCT * upper
                source = source + THROUGH_CONDUCT * value
            if layer < last:
                diagonal = diagonal + THROUGH_CONDUCT
            inverse = 1.0 / diagonal
            upper = THROUGH_CONDUCT * inverse
            value = source * inverse
            slope_ref[layer] = upper
            right_ref[layer] = value
        out_ref[last] = value
        for layer in range(last - 1, -1, -1):
            value = right_ref[layer] + slope_ref[layer] * value
            out_ref[layer] = value

    return pl.pallas_call(
        kernel,
        name="column",
        out_shape=jax.ShapeDtypeStruct(heat_rise.shape, jnp.float32),
        in_specs=[pl.BlockSpec(memory_space=SMEM)] * 2 + [pl.BlockSpec(memory_space=VMEM)] * (6 + hops),
        out_specs=pl.BlockSpec(memory_space=VMEM),
        scratch_shapes=[
            pltpu.SMEM((layers + room,), jnp.int32),
            pltpu.VMEM((chips * each, rows, columns), jnp.float32),
            pltpu.VMEM((layers, rows, columns), jnp.float32),
            pltpu.VMEM((layers, rows, columns), jnp.float32),
        ],
        compiler_params=params(8),
        cost_estimate=pl.CostEstimate(
            flops=200 * layers * rows * columns, bytes_accessed=8 * layers * rows * columns, transcendentals=0
        ),
    )(layer_counts, contacts, *near(heat_rise, other_rise, rise_edge, faces, home, passed, *arrived))


def per_device(shell_conc, heat_rise, layer_current, layer_counts, contacts):
    shell_conc, heat_rise, layer_current = shell_conc[0], heat_rise[0], layer_current[0]
    slots = shell_conc.shape[0]
    layers, part, columns = heat_rise.shape
    devices = lax.axis_size("sub")
    chips = devices // 2
    room = 2 * slots
    contacts = contacts.T
    swap = [(i, i ^ 1) for i in range(devices)]
    other_rise = lax.ppermute(heat_rise, "sub", swap)
    other_rise, current = lax.optimization_barrier((other_rise, layer_current))
    mine, theirs = split_kinetic(shell_conc, current, chips)
    got = lax.ppermute(theirs, "sub", swap)
    *send_rise, send_faces = pack_rise(heat_rise, other_rise, layer_counts, contacts, room)
    *send_kinetic, home = pack_kinetic(mine, got, layer_counts, room)
    send_rise[2:], send_kinetic = lax.optimization_barrier((send_rise[2:], send_kinetic))
    rise = [lax.ppermute(m, "sub", along(hop, chips)) for hop, m in enumerate(send_rise, 1)]
    for i, j in ((0, 2), (1, 1), (2, 0)):
        rise[i], send_kinetic[j] = lax.optimization_barrier((rise[i], send_kinetic[j]))
    kinetic = [lax.ppermute(m, "sub", along(hop, chips)) for hop, m in enumerate(send_kinetic, 1)]
    rise[3], send_faces = lax.optimization_barrier((rise[3], send_faces))
    faces = lax.all_to_all(send_faces, "cell", 0, 0, tiled=True)
    passed_rise = lax.ppermute(pass_rise(rise, layer_counts, slots, room), "sub", swap)
    conc_new = particle(shell_conc, heat_rise, other_rise, rise, passed_rise, layer_current, layer_counts)
    kinetic, faces = lax.optimization_barrier((kinetic, faces))
    passed_kinetic = lax.ppermute(pass_kinetic(kinetic[:-1], conc_new), "sub", swap)
    heat_new = column(
        heat_rise, other_rise, rise[0], home, passed_kinetic, kinetic, faces, layer_counts, contacts
    )
    return conc_new[None], heat_new[None]


def solution(mesh):
    in_specs = (
        P("cell", "sub", None, None, None),
        P("cell", None, "sub", None),
        P("cell", "sub", None, None),
        P(),
        P(),
    )
    out_specs = (P("cell", "sub", None, None, None), P("cell", None, "sub", None))
    return jax.shard_map(
        per_device, mesh=mesh, in_specs=in_specs, out_specs=out_specs, check_vma=False
    )
```
